32 devices in a mesh: groups: 2 (over x), mesh: 16 (over z, y, core).
Axes of the slice: x: 2, y: 2, z: 4, core: 2. Of those that a mesh axis runs over, the one named last changes fastest.
Arguments:
- elem_count: int32 [32], P('groups'), parts along dimension 0, may hold values from 1 to 12, 96 in all
- elem_nodes: int32 [384, 8], P(('groups', 'mesh')), parts along dimension 0, may hold values from 0 to 143, as said below
- bmat: bfloat16 [384, 1152], P(('groups', 'mesh')), parts along dimension 0, may hold values from -4 to 4
- quad_weight: float32 [384, 8], P(('groups', 'mesh')), parts along dimension 0, may hold values from 0.5 to 2
- displacement: float32 [3, 3072], P(None, ('groups', 'mesh')), parts along dimension 1, may hold values from -6 to 6
- load: float32 [3, 3072], P(None, ('groups', 'mesh')), parts along dimension 1, may hold values from -6 to 6
- eps_old: bfloat16 [3072, 6], P(('groups', 'mesh')), parts along dimension 0, may hold values from -5 to 5
- params: bfloat16 [3072, 32], P(('groups', 'mesh')), parts along dimension 0, may hold values from -1 to 1
- hidden: bfloat16 [3072, 512], P(('groups', 'mesh')), parts along dimension 0, may hold values from -0.8984375 to 0.8984375
- sens: bfloat16 [3072, 16384], P(('groups', 'mesh')), parts along dimension 0, may hold values from -4 to 4
- w_x: float32 [38, 1536], replicated, may hold values from -1 to 1
- w_h: bfloat16 [512, 1536], replicated, may hold values from -0.25 to 0.25
- b_x: float32 [1536], replicated, may hold values from -3 to 3
- b_h: float32 [1536], replicated, may hold values from -3 to 3
- w_out: float32 [512, 6], replicated, may hold values from -0.5 to 0.5
- b_out: float32 [6], replicated, may hold values from -3 to 3
Outputs:
- residual: float32 [3, 3072], P(None, ('groups', 'mesh')), parts along dimension 1
- stiffness: float32 [384, 576], P(('groups', 'mesh')), parts along dimension 0
- force_sens: float32 [384, 768], P(('groups', 'mesh')), parts along dimension 0
- hidden_next: bfloat16 [3072, 512], P(('groups', 'mesh')), parts along dimension 0
- sens_next: bfloat16 [3072, 16384], P(('groups', 'mesh')), parts along dimension 0
The draws below stay inside these ranges and needn't reach their ends.
There are 2 independent parts, one for each index of `groups`. The reference program is written for one: setup_inputs(seed, part) draws one part's arguments, and reference() takes and returns one part's arrays. A program takes and returns all parts, laid end to end along the dimension named above; an argument that names none is the same for every part. Nothing has to cross between parts.
Inputs may be any that keep to these rules, and one draw needn't show every extreme that they name: `elem_count`: live elements are the first rows of their partition; the counts sum to 96, and some partition is full. `elem_nodes`: positions index a window of 24 nodes of the previous partition, its own 96 nodes, and 24 nodes of the next; every partition uses the window's first and last position.
All inputs are finite; a program needn't handle non-finite values.
Results may differ from the reference program's by a relative error of at most 0.0057.
Values may be sent and summed in bfloat16 or wider, within the bound.
A program may use at most 128 MiB of HBM per device.

```python
import math
import jax
import jax.numpy as jnp
import numpy as np
from jax import lax

H = 512
NP = 32
NS = 6
NQ = 8
NN = 8
NSUB = 2
E_CAP = 12
E_MEAN = 6
Q_CAP = 96
NODE_DEV = 96
HALO = 24
ELEMS = 192
POINTS = 1536
NODES = 1536
LIVE = 96
N_MESH = 16


def draw_elem_nodes(key, part):
    window = NODE_DEV + 2 * HALO
    nodes = jax.random.randint(key, (N_MESH, E_CAP, NN), 0, window, dtype=jnp.int32)
    nodes = nodes.at[:, 0, 0].set(0)
    nodes = nodes.at[:, 0, NN - 1].set(window - 1)
    return nodes.reshape(N_MESH * E_CAP, NN)


def block_levels(own_key, extent, shards, least, largest):
    level = 1.0
    for position, parts in shards:
        draws = jax.random.uniform(jax.random.fold_in(jax.random.fold_in(own_key, 6), position), (parts,), jnp.float32, least / len(shards), largest / len(shards))
        level = level * jnp.repeat(jnp.exp(draws), extent[position] // parts).reshape((-1,) + (1,) * (len(extent) - 1 - position))
    return level


def length_profile(count, total, bound, lean):
    loads = [(1 << 20) // math.isqrt(grade ** lean) + 1 for grade in range(2, count + 1)]
    surplus, given = total - bound - (count - 1), [1] * (count - 1)
    while surplus > 0:
        candidates = [i for i in range(count - 1) if given[i] < bound]
        mass, left = sum([loads[i] for i in candidates]), surplus
        for i in candidates:
            more = min(bound - given[i], max(1, left * loads[i] // mass), surplus)
            given[i] = given[i] + more
            surplus = surplus - more
    return np.array([bound] + given)


def uneven_parts(own_key, number_of, total, most, skew):
    if number_of == 2:
        one = jax.random.randint(own_key, (), max(1, total - most), min(most, total - 1) + 1)
        return jnp.stack([one, total - one])
    sizes = jnp.asarray(length_profile(number_of, total, most, skew), jnp.int32)
    pairs = (number_of - 1) // 2
    giver, sink = sizes[1:1 + 2 * pairs:2], sizes[2:2 + 2 * pairs:2]
    room = jnp.minimum(giver - 1, most - sink)
    moved = jax.random.randint(jax.random.fold_in(own_key, 1), (pairs,), 0, 1 << 20) % (room + 1)
    sizes = sizes.at[1:1 + 2 * pairs:2].set(giver - moved).at[2:2 + 2 * pairs:2].set(sink + moved)
    return sizes[jax.random.permutation(jax.random.fold_in(own_key, 2), number_of)]


def bell_draw(rng, dims, deviation, most, cuts=(), kind=jnp.bfloat16):
    values = deviation * jax.random.normal(rng, dims, jnp.float32)
    if cuts:
        values = values * block_levels(rng, dims, cuts, -0.22, 0.18)
    return jnp.clip(values, -most, most).astype(kind)


def setup_inputs(seed: int = 0, part: int = 0) -> dict:
    keys = jax.random.split(jax.random.key(seed), 17)
    own_keys = jax.random.split(jax.random.fold_in(keys[16], part), 17)
    elem_count = uneven_parts(own_keys[0], N_MESH, LIVE, E_CAP, 2).astype(jnp.int32)
    elem_nodes = draw_elem_nodes(jax.random.fold_in(jax.random.fold_in(keys[16], part), 71), part)
    bmat = bell_draw(own_keys[2], (ELEMS, NQ * NS * NN * 3), 0.3, 4.0, ((0, 16),))
    quad_weight = jnp.clip(jnp.exp(math.log(2.0) - 1.3862944 * jax.random.uniform(own_keys[3], (ELEMS, NQ), jnp.float32) ** block_levels(own_keys[3], (ELEMS, NQ), ((0, 16),), -0.2, 0.2)), 0.5, 2.0)
    displacement = bell_draw(own_keys[4], (3, NODES), 1.0, 6.0, ((1, 16),), jnp.float32)
    load = bell_draw(own_keys[5], (3, NODES), 1.0, 6.0, ((1, 16),), jnp.float32)
    eps_old = bell_draw(own_keys[6], (POINTS, NS), 1.0, 5.0, ((0, 16),))
    params = jnp.clip(jax.random.uniform(own_keys[7], (POINTS, NP), jnp.float32, -1.0, 1.0) * block_levels(own_keys[7], (POINTS, NP), ((0, 16),), -0.4, 0.0), -1.0, 1.0).astype(jnp.bfloat16)
    hidden = jnp.clip(jax.random.uniform(own_keys[8], (POINTS, H), jnp.float32, -0.8984375, 0.8984375) * block_levels(own_keys[8], (POINTS, H), ((0, 16),), -0.4, 0.0), -0.8984375, 0.8984375).astype(jnp.bfloat16)
    sens = bell_draw(own_keys[9], (POINTS, NP * H), 0.3, 4.0, ((0, 16),))
    w_x = bell_draw(keys[10], (NS + NP, 3 * H), (NS + NP) ** -0.5, 1.0, (), jnp.float32)
    w_h = bell_draw(keys[11], (H, 3 * H), H ** -0.5, 0.25)
    b_x = bell_draw(keys[12], (3 * H,), 0.5, 3.0, (), jnp.float32)
    b_h = bell_draw(keys[13], (3 * H,), 0.5, 3.0, (), jnp.float32)
    w_out = bell_draw(keys[14], (H, NS), (H // 4) ** -0.5, 0.5, (), jnp.float32)
    b_out = bell_draw(keys[15], (NS,), 0.5, 3.0, (), jnp.float32)
    return dict(elem_count=elem_count, elem_nodes=elem_nodes, bmat=bmat, quad_weight=quad_weight, displacement=displacement, load=load, eps_old=eps_old, params=params, hidden=hidden, sens=sens, w_x=w_x, w_h=w_h, b_x=b_x, b_h=b_h, w_out=w_out, b_out=b_out)


HIGHEST = lax.Precision.HIGHEST


def advance(small_block, hidden_block, sens_block, weights):
    w_x, w_h, b_x, b_h, w_out, b_out = weights
    row_count = hidden_block.shape[0]
    width = hidden_block.shape[1]
    param_count = sens_block.shape[1] // width
    strain_count = (small_block.shape[1] - param_count) // 2
    column_count = strain_count + param_count
    floats = small_block.astype(jnp.float32)
    strain_old = floats[:, :strain_count]
    strain_new = floats[:, strain_count:2 * strain_count]
    material = floats[:, 2 * strain_count:]
    tangent = jnp.concatenate([jnp.zeros((row_count, strain_count, width), jnp.bfloat16), sens_block.reshape(row_count, param_count, width)], axis=1)
    state = hidden_block
    for substep in range(NSUB):
        fraction = (substep + 1.0) / NSUB
        drive = jnp.concatenate([strain_old + fraction * (strain_new - strain_old), material], axis=1)
        input_gates = jnp.dot(drive, w_x, precision=HIGHEST) + b_x
        column_scale = jnp.concatenate([jnp.full((strain_count,), fraction, jnp.float32), jnp.ones((param_count,), jnp.float32)])
        input_rates = w_x * column_scale[:, None]
        stacked = jnp.concatenate([state[:, None, :], tangent], axis=1)
        product = jnp.dot(stacked.reshape(row_count * (column_count + 1), width), w_h, preferred_element_type=jnp.float32).reshape(row_count, column_count + 1, 3 * width)
        hidden_gates = product[:, 0, :] + b_h
        hidden_rates = product[:, 1:, :]
        reset = jax.nn.sigmoid(input_gates[:, :width] + hidden_gates[:, :width])
        update = jax.nn.sigmoid(input_gates[:, width:2 * width] + hidden_gates[:, width:2 * width])
        hidden_cand = hidden_gates[:, 2 * width:]
        candidate = jnp.tanh(input_gates[:, 2 * width:] + reset * hidden_cand)
        previous = state.astype(jnp.float32)
        prev_rates = tangent.astype(jnp.float32)
        reset_rate = (reset * (1.0 - reset))[:, None, :] * (input_rates[None, :, :width] + hidden_rates[:, :, :width])
        update_rate = (update * (1.0 - update))[:, None, :] * (input_rates[None, :, width:2 * width] + hidden_rates[:, :, width:2 * width])
        cand_rate = (1.0 - candidate * candidate)[:, None, :] * (input_rates[None, :, 2 * width:] + reset_rate * hidden_cand[:, None, :] + reset[:, None, :] * hidden_rates[:, :, 2 * width:])
        next_state = (1.0 - update) * candidate + update * previous
        next_rates = (1.0 - update)[:, None, :] * cand_rate + update_rate * (previous - candidate)[:, None, :] + update[:, None, :] * prev_rates
        state = next_state.astype(jnp.bfloat16)
        tangent = next_rates.astype(jnp.bfloat16)
    final_state = state.astype(jnp.float32)
    final_rates = tangent.astype(jnp.float32)
    stress = jnp.dot(final_state, w_out, precision=HIGHEST) + b_out
    stress_rates = jnp.einsum('rch,hk->rck', final_rates, w_out, precision=HIGHEST)
    micro_out = jnp.concatenate([stress, stress_rates.reshape(row_count, column_count * strain_count)], axis=1).astype(jnp.bfloat16)
    return state, tangent[:, strain_count:, :].reshape(row_count, param_count * width), micro_out


def advance_rows(small, hidden, sens, weights):
    row_count = hidden.shape[0]
    blocks = row_count // 8

    def advance_block(pieces):
        return advance(pieces[0], pieces[1], pieces[2], weights)

    results = lax.map(advance_block, (small.reshape(blocks, 8, small.shape[1]), hidden.reshape(blocks, 8, hidden.shape[1]), sens.reshape(blocks, 8, sens.shape[1])))
    return tuple(piece.reshape(row_count, piece.shape[2]) for piece in results)


def element_terms(shape_grads, weight, stress, tangent):
    strain_count = stress.shape[2]
    elem_total = stress.shape[0]
    weighted = stress * weight[:, :, None]
    force = jnp.einsum('eqkac,eqk->eac', shape_grads, weighted, precision=HIGHEST)
    strain_rates = tangent[:, :, :strain_count, :] * weight[:, :, None, None]
    left_part = jnp.einsum('eqkac,eqik->eqaci', shape_grads, strain_rates, precision=HIGHEST)
    stiffness = jnp.einsum('eqaci,eqibf->eacbf', left_part, shape_grads, precision=HIGHEST).reshape(elem_total, -1)
    param_rates = tangent[:, :, strain_count:, :] * weight[:, :, None, None]
    force_sens = jnp.einsum('eqkac,eqjk->eacj', shape_grads, param_rates, precision=HIGHEST).reshape(elem_total, -1)
    return force, stiffness, force_sens


def reference(elem_count, elem_nodes, bmat, quad_weight, displacement, load, eps_old, params, hidden, sens, w_x, w_h, b_x, b_h, w_out, b_out):
    weights = (w_x, w_h, b_x, b_h, w_out, b_out)
    point_counts = (elem_count * NQ).astype(jnp.int32)
    starts = (jnp.cumsum(point_counts) - point_counts).astype(jnp.int32)
    live_total = N_MESH * NQ * E_MEAN
    positions = jnp.arange(live_total, dtype=jnp.int32)
    owner = (jnp.sum((starts[None, :] <= positions[:, None]).astype(jnp.int32), axis=1) - 1).astype(jnp.int32)
    slot_index = (owner * Q_CAP + positions - starts[owner]).astype(jnp.int32)
    padded = jnp.pad(displacement, ((0, 0), (HALO, HALO)))
    partition = (jnp.arange(ELEMS, dtype=jnp.int32) // E_CAP).astype(jnp.int32)
    global_nodes = (partition[:, None] * NODE_DEV + elem_nodes).astype(jnp.int32)
    node_values = padded[:, global_nodes]
    shape_grads = bmat.astype(jnp.float32).reshape(ELEMS, NQ, NS, NN, 3)
    strain = jnp.einsum('eqkac,cea->eqk', shape_grads, node_values, precision=HIGHEST).reshape(POINTS, NS).astype(jnp.bfloat16)
    small = jnp.concatenate([eps_old, strain, params], axis=1)
    picked = advance_rows(small[slot_index], hidden[slot_index], sens[slot_index], weights)
    hidden_next = jnp.zeros((POINTS, H), jnp.bfloat16).at[slot_index].set(picked[0])
    sens_next = jnp.zeros((POINTS, NP * H), jnp.bfloat16).at[slot_index].set(picked[1])
    micro_out = jnp.zeros((POINTS, picked[2].shape[1]), jnp.bfloat16).at[slot_index].set(picked[2])
    micro_floats = micro_out.astype(jnp.float32)
    stress = micro_floats[:, :NS].reshape(ELEMS, NQ, NS)
    tangent = micro_floats[:, NS:].reshape(ELEMS, NQ, NS + NP, NS)
    force, stiffness, force_sens = element_terms(shape_grads, quad_weight, stress, tangent)
    element_live = (jnp.arange(ELEMS, dtype=jnp.int32) - partition * E_CAP) < elem_count[partition]
    force = jnp.where(element_live[:, None, None], force, 0.0)
    stiffness = jnp.where(element_live[:, None], stiffness, 0.0)
    force_sens = jnp.where(element_live[:, None], force_sens, 0.0)
    assembled = jnp.zeros((3, NODES + 2 * HALO), jnp.float32).at[:, global_nodes.reshape(-1)].add(force.reshape(-1, 3).T)
    residual = load - assembled[:, HALO:HALO + NODES]
    return (residual, stiffness, force_sens, hidden_next, sens_next)
```

```python
import jax
import jax.numpy as jnp
import numpy as np
from jax import lax
from jax.experimental import pallas as pl
from jax.experimental.pallas import tpu as pltpu
from jax.sharding import PartitionSpec as P

NSUB = 2
GROUP = 4
HIGHEST = lax.Precision.HIGHEST
BF = jnp.bfloat16
F32 = jnp.float32


def dot(x, y):
    return jnp.dot(x, y, preferred_element_type=F32)


def split(x):
    high = x.astype(BF)
    return high, (x - high.astype(F32)).astype(BF)


def constants(elems, quads, strains, nodes, params):
    span = nodes * 3
    wide = strains * span
    lane = np.arange(wide)
    k, ac = lane // span, lane % span
    a, c = ac // 3, ac % 3
    points = elems * quads
    out = np.arange(span * span)
    left = ac[:, None] == (out // span)[None, :]
    right = ac[:, None] == (out % span)[None, :]
    cols = np.arange(span * params)
    sens = ac[:, None] == (cols // params)[None, :]
    rows = -(-elems // 16) * 16
    total = np.arange(rows)[:, None] == (np.arange(points) // quads)[None, :]
    of_strain = k[:, None] == np.arange(strains)[None, :]
    spread = np.arange(strains)[:, None] == k[None, :]
    direction = np.arange(3)[:, None] == c[None, :]
    force = (np.arange(nodes * 8)[:, None] == (a * 8 + c)[None, :])
    bf = [m.astype(BF) for m in (left, right, sens, total, of_strain, spread, direction, force)]
    ints = [
        a.astype(np.int32)[None, :],
        k.astype(np.int32)[None, :],
        (cols % params).astype(np.int32)[None, :],
    ]
    return [jnp.asarray(m) for m in bf + ints]


def body(
    count_ref, u_ref, nodes_ref, b_ref, qw_ref, eps_ref, par_ref, hid_ref,
    wx_ref, wh_ref, bx_ref, bh_ref, wo_ref, bo_ref,
    left_ref, right_ref, sensm_ref, total_ref, ofk_ref, spread_ref, dir_ref, forcem_ref,
    la_ref, lk_ref, lj_ref,
    sens_ref,
    wide_ref, stiff_ref, fs_ref, hn_ref, sn_ref,
    coef, wrep, wb, d1, d2, rsum, gs, onehot,
):
    step = pl.program_id(0)
    last = pl.num_programs(0) - 1
    points, width = hid_ref.shape
    elems = stiff_ref.shape[0]
    quads = points // elems
    strains = eps_ref.shape[1]
    node_each = nodes_ref.shape[1]
    window = u_ref.shape[0]
    rows16 = total_ref.shape[0]
    param_count = par_ref.shape[1]
    live = count_ref[lax.axis_index("mesh")] * quads
    half = width // 2

    def rates(stacked, columns, sub, rates_of, old_of, put):
        for jt in range(2):
            lo = jt * half
            if stacked is not None:
                pr = dot(stacked, wh_ref[:, lo : lo + half])
                pz = dot(stacked, wh_ref[:, width + lo : width + lo + half])
                pn = dot(stacked, wh_ref[:, 2 * width + lo : 2 * width + lo + half])
            for pt in range(points // 16):
                at = slice(pt * 16, pt * 16 + 16)
                ca, cb, cc, cr, cz = [coef[sub, i, at, lo : lo + half] for i in range(5)]
                for g in range(columns):
                    rows = slice(g * points + pt * 16, g * points + pt * 16 + 16)
                    vr = rates_of(g, lo)
                    vz = rates_of(g, width + lo)
                    vn = rates_of(g, 2 * width + lo)
                    if stacked is None:
                        new = cb * vr + cc * vz + ca * vn
                    else:
                        new = (
                            cb * (vr + pr[rows])
                            + cc * (vz + pz[rows])
                            + ca * (vn + cr * pn[rows])
                            + cz * old_of(g, at, lo).astype(F32)
                        )
                    put(g, at, lo, new)

    def point_terms(stacked, columns):
        t = dot(stacked, wrep[...]).astype(BF).astype(F32)
        return [(t[g * points : (g + 1) * points] * wb[...]).astype(BF) for g in range(columns)]

    @pl.when(step == 0)
    def _():
        alive = lax.broadcasted_iota(jnp.int32, (points, 1), 0) < live
        b = b_ref[...].astype(F32)
        wb[...] = jnp.where(alive, b * qw_ref[...], 0.0)
        wrep[...] = dot(wo_ref[...].astype(BF), spread_ref[...]).astype(BF)
        node = lax.broadcasted_iota(jnp.int32, (points, window), 1)
        for a in range(node_each):
            hit = jnp.where(nodes_ref[:, a : a + 1] == node, 1.0, 0.0)
            onehot[a * points : (a + 1) * points, :] = hit.astype(BF)
        u_high, u_low = split(u_ref[...])
        spread_high = dot(u_high, dir_ref[...]).astype(BF)
        spread_low = dot(u_low, dir_ref[...]).astype(BF)
        values = dot(onehot[...], spread_high) + dot(onehot[...], spread_low)
        mine = jnp.zeros((points, values.shape[1]), F32)
        for a in range(node_each):
            mine += jnp.where(la_ref[...] == a, values[a * points : (a + 1) * points], 0.0)
        high, low = split(b * mine)
        strain = (dot(high, ofk_ref[...]) + dot(low, ofk_ref[...])).astype(BF).astype(F32)
        eps = eps_ref[...].astype(F32)
        material = jnp.dot(
            par_ref[...].astype(F32), wx_ref[strains : strains + param_count, :],
            precision=HIGHEST, preferred_element_type=F32,
        ) + bx_ref[...]
        state = hid_ref[...]
        for sub in range(NSUB):
            fraction = (sub + 1.0) / NSUB
            drive = eps + fraction * (strain - eps)
            gx = material + jnp.dot(
                drive, wx_ref[0:strains, :], precision=HIGHEST, preferred_element_type=F32
            )
            gh = dot(state, wh_ref[...]) + bh_ref[...]
            reset = jax.nn.sigmoid(gx[:, :width] + gh[:, :width])
            update = jax.nn.sigmoid(gx[:, width : 2 * width] + gh[:, width : 2 * width])
            cand_h = gh[:, 2 * width :]
            cand = jnp.tanh(gx[:, 2 * width :] + reset * cand_h)
            previous = state.astype(F32)
            ca = (1.0 - update) * (1.0 - cand * cand)
            coef[sub, 0] = ca
            coef[sub, 1] = ca * cand_h * (reset * (1.0 - reset))
            coef[sub, 2] = (previous - cand) * (update * (1.0 - update))
            coef[sub, 3] = reset
            coef[sub, 4] = update
            state = ((1.0 - update) * cand + update * previous).astype(BF)
        hn_ref[...] = jnp.where(alive, state.astype(F32), 0.0).astype(BF)
        stress = (dot(state, wrep[...]) + dot(bo_ref[...], spread_ref[...].astype(F32)))
        high, low = split(stress.astype(BF).astype(F32) * wb[...])
        dims = (((1,), (1,)), ((), ()))
        by_point = lax.dot_general(forcem_ref[...], high, dims, preferred_element_type=F32)
        by_point += lax.dot_general(forcem_ref[...], low, dims, preferred_element_type=F32)
        high, low = split(by_point)
        wide = jnp.zeros((8, window), F32)
        for a in range(node_each):
            hot = onehot[a * points : (a + 1) * points, :]
            wide += dot(high[a * 8 : a * 8 + 8], hot) + dot(low[a * 8 : a * 8 + 8], hot)
        wide_ref[...] = wide

    def sens_rate(g, lane):
        return wx_ref[pl.ds(strains + step * GROUP + g, 1), lane : lane + half]

    def put_first(g, at, lo, new):
        d1[pl.ds(g * points + at.start, 16), lo : lo + half] = new.astype(BF)

    def put_last(g, at, lo, new):
        d2[pl.ds(g * points + at.start, 16), lo : lo + half] = new.astype(BF)
        alive = lax.broadcasted_iota(jnp.int32, (16, 1), 0) + at.start < live
        sn_ref[at, g * width + lo : g * width + lo + half] = jnp.where(alive, new, 0.0).astype(BF)

    stacked = jnp.concatenate(
        [sens_ref[:, g * width : (g + 1) * width] for g in range(GROUP)], axis=0
    )
    rates(
        stacked, GROUP, 0, sens_rate,
        lambda g, at, lo: sens_ref[at, g * width + lo : g * width + lo + half], put_first,
    )
    many = GROUP * points
    rates(
        d1[0:many, :], GROUP, 1, sens_rate,
        lambda g, at, lo: d1[g * points + at.start : g * points + at.stop, lo : lo + half],
        put_last,
    )
    for g, piece in enumerate(point_terms(d2[0:many, :], GROUP)):
        where = pl.multiple_of((step * GROUP + g) * rows16, rows16)
        rsum[pl.ds(where, rows16), :] = dot(total_ref[...], piece).astype(BF)

    @pl.when(step == last)
    def _():
        def strain_rate(scale):
            return lambda g, lane: wx_ref[g : g + 1, lane : lane + half] * scale

        def put_second(g, at, lo, new):
            d2[pl.ds(g * points + at.start, 16), lo : lo + half] = new.astype(BF)

        some = strains * points
        rates(None, strains, 0, strain_rate(1.0 / NSUB), None, put_first)
        rates(
            d1[0:some, :], strains, 1, strain_rate(1.0),
            lambda g, at, lo: d1[g * points + at.start : g * points + at.stop, lo : lo + half],
            put_second,
        )
        for i, piece in enumerate(point_terms(d2[0:some, :], strains)):
            gs[i * points : (i + 1) * points, :] = piece
        b = b_ref[...].astype(F32)
        acc = jnp.zeros((points, stiff_ref.shape[1]), F32)
        for i in range(strains):
            one = jnp.where(lk_ref[...] == i, b, 0.0).astype(BF)
            acc += dot(gs[i * points : (i + 1) * points, :], left_ref[...]) * dot(
                one, right_ref[...]
            )
        stiff_ref[...] = jnp.sum(acc.reshape(elems, quads, acc.shape[1]), axis=1)
        placed = dot(rsum[...], sensm_ref[...])
        fs = jnp.zeros((rows16, fs_ref.shape[1]), F32)
        for j in range(param_count):
            fs += jnp.where(lj_ref[...] == j, placed[j * rows16 : (j + 1) * rows16], 0.0)
        fs_ref[...] = fs[:elems]


def on_device(
    elem_count, elem_nodes, bmat, quad_weight, displacement, load, eps_old, params,
    hidden, sens, w_x, w_h, b_x, b_h, w_out, b_out,
):
    elems, node_each = elem_nodes.shape
    quads = quad_weight.shape[1]
    points, strains = eps_old.shape
    param_count = params.shape[1]
    width = hidden.shape[1]
    owned = displacement.shape[1]
    halo = owned // 4
    window = owned + 2 * halo
    wide = strains * node_each * 3
    peers = lax.axis_size("mesh")
    up = [(i, i + 1) for i in range(peers - 1)]
    down = [(i + 1, i) for i in range(peers - 1)]
    before = lax.ppermute(displacement[:, owned - halo :], "mesh", up)
    after = lax.ppermute(displacement[:, :halo], "mesh", down)
    u = jnp.concatenate([before, displacement, after], axis=1).T
    nodes = jnp.repeat(elem_nodes, quads, axis=0)
    consts = constants(elems, quads, strains, node_each, param_count)
    rows16 = consts[3].shape[0]
    operands = [
        u, nodes, bmat.reshape(points, wide), quad_weight.reshape(points, 1), eps_old, params,
        hidden, w_x, w_h, b_x[None], b_h[None], w_out, b_out[None], *consts,
    ]
    columns = max(GROUP, strains)

    def whole(x):
        return pl.BlockSpec(x.shape, lambda i: (0, 0))

    def const_out(shape):
        return pl.BlockSpec(shape, lambda i: (0, 0))

    streamed = pl.BlockSpec((points, GROUP * width), lambda i: (0, i))
    span = node_each * 3
    force, stiffness, force_sens, hidden_next, sens_next = pl.pallas_call(
        body,
        grid=(param_count // GROUP,),
        in_specs=[pl.BlockSpec(memory_space=pltpu.SMEM)] + [whole(x) for x in operands] + [streamed],
        out_specs=[
            const_out((8, window)), const_out((elems, span * span)),
            const_out((elems, span * param_count)), const_out((points, width)), streamed,
        ],
        out_shape=[
            jax.ShapeDtypeStruct((8, window), F32),
            jax.ShapeDtypeStruct((elems, span * span), F32),
            jax.ShapeDtypeStruct((elems, span * param_count), F32),
            jax.ShapeDtypeStruct((points, width), BF),
            jax.ShapeDtypeStruct(sens.shape, BF),
        ],
        scratch_shapes=[
            pltpu.VMEM((NSUB, 5, points, width), F32),
            pltpu.VMEM((width, wide), BF),
            pltpu.VMEM((points, wide), F32),
            pltpu.VMEM((columns * points, width), BF),
            pltpu.VMEM((columns * points, width), BF),
            pltpu.VMEM((param_count * rows16, wide), BF),
            pltpu.VMEM((strains * points, wide), BF),
            pltpu.VMEM((node_each * points, window), BF),
        ],
        compiler_params=pltpu.CompilerParams(vmem_limit_bytes=48 << 20),
    )(elem_count, *operands, sens)
    force = force[:3]
    from_right = lax.ppermute(force[:, :halo], "mesh", down)
    from_left = lax.ppermute(force[:, halo + owned :], "mesh", up)
    mid = force[:, halo : halo + owned]
    gap = jnp.zeros((3, owned - halo), F32)
    residual = load - (
        mid
        + jnp.concatenate([gap, from_right], axis=1)
        + jnp.concatenate([from_left, gap], axis=1)
    )
    return (residual, stiffness, force_sens, hidden_next, sens_next)


def solution(mesh):
    both = ("groups", "mesh")
    rows, cols = P(both, None), P(None, both)
    return jax.shard_map(
        on_device,
        mesh=mesh,
        in_specs=(P("groups"), rows, rows, rows, cols, cols) + (rows,) * 4 + (P(),) * 6,
        out_specs=(cols, rows, rows, rows, rows),
        check_vma=False,
    )
```

```python
import jax
import jax.numpy as jnp
from jax import lax
from jax.experimental import pallas as pl
from jax.experimental.pallas import tpu as pltpu
from jax.sharding import PartitionSpec as P

NSUB = 2
GROUP = 4
FIRST_VMEM = 60 << 20
SECOND_VMEM = 60 << 20
HIGHEST = lax.Precision.HIGHEST
BF = jnp.bfloat16
F32 = jnp.float32


def dot(x, y):
    return jnp.dot(x, y, preferred_element_type=F32)


def split(x):
    high = x.astype(BF)
    return high, (x - high.astype(F32)).astype(BF)


def turned(x, y, precision=None):
    dims = (((1,), (1,)), ((), ()))
    return lax.dot_general(x, y, dims, precision=precision, preferred_element_type=F32)


def upright(x, y, precision=None):
    dims = (((0,), (0,)), ((), ()))
    return lax.dot_general(x, y, dims, precision=precision, preferred_element_type=F32)


def iota(shape, dim):
    return lax.broadcasted_iota(jnp.int32, shape, dim)


def over(x, d):
    return (x * -(-65536 // d)) >> 16


def within(x, d):
    return x - over(x, d) * d


def where_one(mask):
    return jnp.where(mask, 1.0, 0.0).astype(BF)


def advance_rates(coef, wh_ref, points, width):
    half = width // 2

    def rates(stacked, columns, sub, rates_of, old_of, put):
        for jt in range(2):
            lo = jt * half
            if stacked is not None:
                pr = dot(stacked, wh_ref[:, lo : lo + half])
                pz = dot(stacked, wh_ref[:, width + lo : width + lo + half])
                pn = dot(stacked, wh_ref[:, 2 * width + lo : 2 * width + lo + half])
            for pt in range(points // 16):
                at = slice(pt * 16, pt * 16 + 16)
                ca, cb, cc, cr, cz = [coef[sub, i, at, lo : lo + half] for i in range(5)]
                for g in range(columns):
                    rows = slice(g * points + pt * 16, g * points + pt * 16 + 16)
                    vr = rates_of(g, lo)
                    vz = rates_of(g, width + lo)
                    vn = rates_of(g, 2 * width + lo)
                    if stacked is None:
                        new = cb * vr + cc * vz + ca * vn
                    else:
                        new = (
                            cb * (vr + pr[rows])
                            + cc * (vz + pz[rows])
                            + ca * (vn + cr * pn[rows])
                            + cz * old_of(g, at, lo).astype(F32)
                        )
                    put(g, at, lo, new)


    return rates


def point_terms(stacked, columns, points, wrep, wb):
    t = dot(stacked, wrep[...]).astype(BF).astype(F32)
    return [(t[g * points : (g + 1) * points] * wb[...]).astype(BF) for g in range(columns)]


def first(
    count_ref, disp_ref, load_ref, nodes_ref, bmat_ref, qw_ref, eps_ref, par_ref, hid_ref,
    wx_ref, wh_ref, bx_ref, bh_ref, wo_ref, bo_ref,
    res_ref, coef, gs, wb, wrep, b96, state_ref,
    d1, d2, onehot, mine_u, got_u, part, got_f, send_sem, recv_sem,
):
    peers = lax.axis_size("mesh")
    me = lax.axis_index("mesh")
    right, left = lax.rem(me + 1, peers), lax.rem(me + peers - 1, peers)
    barrier = pltpu.get_barrier_semaphore()
    for other in (left, right):
        pl.semaphore_signal(
            barrier, inc=1, device_id={"mesh": other}, device_id_type=pl.DeviceIdType.MESH
        )
    points, width = hid_ref.shape
    node_each, elems = nodes_ref.shape
    quads = points // elems
    strains = eps_ref.shape[0]
    param_count = par_ref.shape[0]
    owned = disp_ref.shape[1]
    halo = owned // 4
    span = node_each * 3
    wide = strains * span
    half = width // 2
    live = count_ref[me] * quads

    def send(src, dst, i, other):
        copy = pltpu.make_async_remote_copy(
            src_ref=src, dst_ref=dst, send_sem=send_sem.at[i], recv_sem=recv_sem.at[i],
            device_id={"mesh": other}, device_id_type=pl.DeviceIdType.MESH,
        )
        copy.start()
        return copy

    mine_u[...] = jnp.zeros_like(mine_u)
    mine_u[0:3, 0:owned] = disp_ref[...]
    pl.semaphore_wait(barrier, 2)
    to_right = send(mine_u, got_u.at[0], 0, right)
    to_left = send(mine_u, got_u.at[1], 1, left)

    alive = iota((points, 1), 0) < live
    by_elem = over(iota((points, elems), 0), quads) == iota((points, elems), 1)
    rep = where_one(by_elem)
    rep32 = jnp.where(by_elem, 1.0, 0.0)
    nodes = turned(rep32, nodes_ref[...].astype(F32), HIGHEST)
    weights = turned(rep32, qw_ref[...], HIGHEST)
    mine_q = within(iota((points, quads), 0), quads) == iota((points, quads), 1)
    weight = jnp.sum(jnp.where(mine_q, weights, 0.0), axis=1, keepdims=True)
    rows = dot(rep, bmat_ref[...])
    b = jnp.zeros((points, wide), F32)
    which = within(iota((points, 1), 0), quads)
    for q in range(quads):
        b += jnp.where(which == q, rows[:, q * wide : (q + 1) * wide], 0.0)
    b96[...] = b.astype(BF)
    wb[...] = jnp.where(alive, b * weight, 0.0)
    spread = where_one(over(iota((strains, wide), 1), span) == iota((strains, wide), 0))
    wrep[...] = upright(wo_ref[...].astype(BF), spread).astype(BF)
    nodes = jnp.where(
        nodes < halo,
        nodes + (owned - halo),
        jnp.where(nodes < halo + owned, nodes + (128 - halo), nodes + (256 - halo - owned)),
    )
    node = iota((points, 384), 1).astype(F32)
    for a in range(node_each):
        onehot[a * points : (a + 1) * points, :] = where_one(
            jnp.abs(nodes[:, a : a + 1] - node) < 0.5
        )
    material = upright(
        par_ref[...].astype(F32), wx_ref[strains : strains + param_count, :], HIGHEST
    ) + bx_ref[...].reshape(1, 3 * width)
    state = hid_ref[...]
    gh = dot(state, wh_ref[...])
    b_h = bh_ref[...].reshape(1, 3 * width)

    to_right.wait()
    to_left.wait()
    from_left = jnp.where(me > 0, 1.0, 0.0)
    from_right = jnp.where(me < peers - 1, 1.0, 0.0)
    u = jnp.concatenate([got_u[0] * from_left, mine_u[...], got_u[1] * from_right], axis=1)
    u_high, u_low = split(u)
    at_nodes = turned(onehot[...], jnp.concatenate([u_high, u_low], axis=0)).astype(BF)
    lane = within(iota((16, wide), 1), span)
    direction = where_one(within(lane, 3) == jnp.bitwise_and(iota((16, wide), 0), 7))
    values = dot(at_nodes, direction)
    which = over(within(iota((1, wide), 1), span), 3)
    mine = jnp.zeros((points, wide), F32)
    for a in range(node_each):
        mine += jnp.where(which == a, values[a * points : (a + 1) * points], 0.0)
    high, low = split(b * mine)
    strain = (turned(spread, high) + turned(spread, low)).astype(BF).astype(F32)
    eps = eps_ref[...].astype(F32)
    for sub in range(NSUB):
        fraction = (sub + 1.0) / NSUB
        drive = eps + fraction * (strain - eps)
        gx = material + upright(drive, wx_ref[0:strains, :], HIGHEST)
        if sub:
            gh = dot(state, wh_ref[...])
        gh = gh + b_h
        reset = jax.nn.sigmoid(gx[:, :width] + gh[:, :width])
        update = jax.nn.sigmoid(gx[:, width : 2 * width] + gh[:, width : 2 * width])
        cand_h = gh[:, 2 * width :]
        cand = jnp.tanh(gx[:, 2 * width :] + reset * cand_h)
        previous = state.astype(F32)
        ca = (1.0 - update) * (1.0 - cand * cand)
        coef[sub, 0] = ca
        coef[sub, 1] = ca * cand_h * (reset * (1.0 - reset))
        coef[sub, 2] = (previous - cand) * (update * (1.0 - update))
        coef[sub, 3] = reset
        coef[sub, 4] = update
        state = ((1.0 - update) * cand + update * previous).astype(BF)
    state_ref[...] = jnp.where(alive, state.astype(F32), 0.0).astype(BF)
    stress = dot(state, wrep[...]) + dot(bo_ref[...], spread.astype(F32))
    high, low = split(stress.astype(BF).astype(F32) * wb[...])
    shape = (node_each * 8, wide)
    lane = within(iota(shape, 1), span)
    node_row = iota(shape, 0)
    placed = where_one(over(lane, 3) * 8 + within(lane, 3) == node_row)
    by_point = turned(placed, high) + turned(placed, low)
    high, low = split(by_point)
    total = jnp.zeros((8, 384), F32)
    for a in range(node_each):
        hot = onehot[a * points : (a + 1) * points, :]
        total += dot(high[a * 8 : a * 8 + 8], hot) + dot(low[a * 8 : a * 8 + 8], hot)
    for i in range(3):
        part[i] = total[:, i * 128 : (i + 1) * 128]
    to_left = send(part.at[0], got_f.at[1], 2, left)
    to_right = send(part.at[2], got_f.at[0], 3, right)

    rates = advance_rates(coef, wh_ref, points, width)

    def strain_rate(scale):
        return lambda g, lane: wx_ref[g : g + 1, lane : lane + half] * scale

    def put(into):
        def store(g, at, lo, new):
            into[g * points + at.start : g * points + at.stop, lo : lo + half] = new.astype(BF)

        return store

    rates(None, strains, 0, strain_rate(1.0 / NSUB), None, put(d1))
    rates(
        d1[...], strains, 1, strain_rate(1.0),
        lambda g, at, lo: d1[g * points + at.start : g * points + at.stop, lo : lo + half],
        put(d2),
    )
    for i, piece in enumerate(point_terms(d2[...], strains, points, wrep, wb)):
        gs[i * points : (i + 1) * points, :] = piece
    to_left.wait()
    to_right.wait()
    force = part[1] + got_f[0] * from_left + got_f[1] * from_right
    res_ref[...] = load_ref[...] - force[0:3, 0:owned]


def second(
    count_ref, coef, gs, wb, wrep, b96, state_ref, wx_ref, wh_ref, sens_ref,
    stiff_ref, fs_ref, hn_ref, sn_ref,
    d1, d2, rsum,
):
    step = pl.program_id(0)
    last = pl.num_programs(0) - 1
    points, width = state_ref.shape
    elems = stiff_ref.shape[0]
    quads = points // elems
    strains = gs.shape[0] // points
    wide = wb.shape[1]
    span = wide // strains
    param_count = wx_ref.shape[0] - strains
    rows16 = rsum.shape[0] // param_count
    half = width // 2
    live = count_ref[lax.axis_index("mesh")] * quads
    total = where_one(over(iota((rows16, points), 1), quads) == iota((rows16, points), 0))
    rates = advance_rates(coef, wh_ref, points, width)

    def sens_rate(g, lane):
        return wx_ref[pl.ds(strains + step * GROUP + g, 1), lane : lane + half]

    def put_first(g, at, lo, new):
        d1[g * points + at.start : g * points + at.stop, lo : lo + half] = new.astype(BF)

    def put_last(g, at, lo, new):
        d2[g * points + at.start : g * points + at.stop, lo : lo + half] = new.astype(BF)
        alive = iota((16, 1), 0) + at.start < live
        sn_ref[at, g * width + lo : g * width + lo + half] = jnp.where(alive, new, 0.0).astype(BF)

    stacked = jnp.concatenate(
        [sens_ref[:, g * width : (g + 1) * width] for g in range(GROUP)], axis=0
    )
    rates(
        stacked, GROUP, 0, sens_rate,
        lambda g, at, lo: sens_ref[at, g * width + lo : g * width + lo + half], put_first,
    )
    rates(
        d1[...], GROUP, 1, sens_rate,
        lambda g, at, lo: d1[g * points + at.start : g * points + at.stop, lo : lo + half],
        put_last,
    )
    for g, piece in enumerate(point_terms(d2[...], GROUP, points, wrep, wb)):
        where = pl.multiple_of((step * GROUP + g) * rows16, rows16)
        rsum[pl.ds(where, rows16), :] = dot(total, piece).astype(BF)

    @pl.when(step == last)
    def _():
        hn_ref[...] = state_ref[...]
        b = b96[...].astype(F32)
        shape = (wide, span * span)
        ac, out = within(iota(shape, 0), span), iota(shape, 1)
        to_left = where_one(ac == over(out, span))
        to_right = where_one(ac == within(out, span))
        of = over(iota((1, wide), 1), span)
        acc = jnp.zeros((points, span * span), F32)
        for i in range(strains):
            one = jnp.where(of == i, b, 0.0).astype(BF)
            acc += dot(gs[i * points : (i + 1) * points, :], to_left) * dot(one, to_right)
        stiff_ref[...] = jnp.sum(acc.reshape(elems, quads, span * span), axis=1)
        shape = (wide, span * param_count)
        spread = where_one(within(iota(shape, 0), span) == over(iota(shape, 1), param_count))
        placed = dot(rsum[...], spread)
        fs = jnp.zeros((rows16, span * param_count), F32)
        of = within(iota((1, span * param_count), 1), param_count)
        for j in range(param_count):
            fs += jnp.where(of == j, placed[j * rows16 : (j + 1) * rows16], 0.0)
        fs_ref[...] = fs[:elems]


def on_device(
    elem_count, elem_nodes, bmat, quad_weight, displacement, load, eps_old, params,
    hidden, sens, w_x, w_h, b_x, b_h, w_out, b_out,
):
    elems, node_each = elem_nodes.shape
    points, strains = eps_old.shape
    param_count = params.shape[1]
    width = hidden.shape[1]
    span = node_each * 3
    wide = strains * span
    rows16 = -(-elems // 16) * 16
    smem = pl.BlockSpec(memory_space=pltpu.SMEM)
    vmem = pl.BlockSpec(memory_space=pltpu.VMEM)
    operands = [
        displacement, load, elem_nodes.T, bmat, quad_weight.T, eps_old.T, params.T, hidden,
        w_x, w_h, b_x, b_h, w_out.T, b_out[None],
    ]
    residual, coef, gs, wb, wrep, b96, state = pl.pallas_call(
        first,
        in_specs=[smem] + [vmem] * len(operands),
        out_specs=[vmem] * 7,
        out_shape=[
            jax.ShapeDtypeStruct(load.shape, F32),
            jax.ShapeDtypeStruct((NSUB, 5, points, width), F32),
            jax.ShapeDtypeStruct((strains * points, wide), BF),
            jax.ShapeDtypeStruct((points, wide), F32),
            jax.ShapeDtypeStruct((width, wide), BF),
            jax.ShapeDtypeStruct((points, wide), BF),
            jax.ShapeDtypeStruct((points, width), BF),
        ],
        scratch_shapes=[
            pltpu.VMEM((strains * points, width), BF),
            pltpu.VMEM((strains * points, width), BF),
            pltpu.VMEM((node_each * points, 384), BF),
            pltpu.VMEM((8, 128), F32),
            pltpu.VMEM((2, 8, 128), F32),
            pltpu.VMEM((3, 8, 128), F32),
            pltpu.VMEM((2, 8, 128), F32),
            pltpu.SemaphoreType.DMA((4,)),
            pltpu.SemaphoreType.DMA((4,)),
        ],
        compiler_params=pltpu.CompilerParams(
            vmem_limit_bytes=FIRST_VMEM, collective_id=0, has_side_effects=True
        ),
    )(elem_count, *operands)

    def whole(x):
        return pl.BlockSpec(x.shape, lambda i: (0,) * x.ndim)

    streamed = pl.BlockSpec((points, GROUP * width), lambda i: (0, i))
    outs = [
        jax.ShapeDtypeStruct((elems, span * span), F32),
        jax.ShapeDtypeStruct((elems, span * param_count), F32),
        jax.ShapeDtypeStruct((points, width), BF),
    ]
    operands = [coef, gs, wb, wrep, b96, state, w_x, w_h]
    stiffness, force_sens, hidden_next, sens_next = pl.pallas_call(
        second,
        grid=(param_count // GROUP,),
        in_specs=[smem] + [whole(x) for x in operands] + [streamed],
        out_specs=[whole(x) for x in outs] + [streamed],
        out_shape=outs + [jax.ShapeDtypeStruct(sens.shape, BF)],
        scratch_shapes=[
            pltpu.VMEM((GROUP * points, width), BF),
            pltpu.VMEM((GROUP * points, width), BF),
            pltpu.VMEM((param_count * rows16, wide), BF),
        ],
        compiler_params=pltpu.CompilerParams(vmem_limit_bytes=SECOND_VMEM),
    )(elem_count, *operands, sens)
    return (residual, stiffness, force_sens, hidden_next, sens_next)


def solution(mesh):
    both = ("groups", "mesh")
    rows, cols = P(both, None), P(None, both)
    return jax.shard_map(
        on_device,
        mesh=mesh,
        in_specs=(P("groups"), rows, rows, rows, cols, cols) + (rows,) * 4 + (P(),) * 6,
        out_specs=(cols, rows, rows, rows, rows),
        check_vma=False,
    )
```
